256 devices in a mesh: freq: 8 (over z_hi, y), sy: 8 (over z_lo, core), sx: 4 (over x).
Axes of the slice: x: 4, y: 4, z: 8 (z_hi: 2, z_lo: 4; z = z_hi * 4 + z_lo), core: 2. Of those that a mesh axis runs over, the one named last changes fastest.
Arguments:
- cube: bfloat16 [1024, 128, 512], P('freq', 'sy', 'sx')
- pos_embed: bfloat16 [1024, 768], replicated, may hold values from -3 to 3
- w_in: bfloat16 [256, 768], replicated, may hold values from -0.375 to 0.375
- norm_gain: float32 [768], replicated, may hold values from 0.5 to 1.5
- w_query: bfloat16 [768, 768], replicated, may hold values from -0.21875 to 0.21875
- w_key: bfloat16 [768, 768], replicated, may hold values from -0.21875 to 0.21875
- w_value: bfloat16 [768, 768], replicated, may hold values from -0.21875 to 0.21875
- w_out: bfloat16 [768, 768], replicated, may hold values from -0.21875 to 0.21875
- attn_scale: float32 [12], replicated, may hold values from 3 to 30
- w_proj: bfloat16 [768, 512], replicated, may hold values from -0.21875 to 0.21875
- mix_weight: float32 [3, 3, 512], replicated, may hold values from -2 to 2
- optical: bfloat16 [1024, 512], P(('freq', 'sy', 'sx'))
- logit_scale: float32 [1], replicated, may hold values from 40 to 50
- pattern: int32 [8, 4, 8, 8, 3], P('sy', 'sx', 'freq'), may hold values from 0 to 7, as said below
- match_ids: int32 [8, 4, 8], P('sy', 'sx', 'freq'), may hold values from 0 to 1023, as said below
Outputs:
- layer_out: bfloat16 [8, 4, 8, 1024, 768], P('sy', 'sx', 'freq')
- embed: float32 [8, 4, 8, 512], P('sy', 'sx', 'freq')
- block_loss: float32 [8, 4, 8], P('sy', 'sx', 'freq')
The draws below stay inside these ranges and needn't reach their ends.
Inputs may be any that keep to these rules, and one draw needn't show every extreme that they name: `pattern`: for every pixel block and query block, the 3 key block indices are distinct. `match_ids`: counting devices on freq+sy+sx with freq slowest, the block of device d = f * 8 * 4 + i * 4 + j has its counterpart among the 4 candidates of device (d + 128) mod 256.
All inputs are finite; a program needn't handle non-finite values.
Results may differ from the reference program's by a relative error of at most 0.012.
The reference program's roundings to bfloat16 on the way count: a program that leaves them out, or rounds other values in their place, can miss the bound.
Values may be sent and summed in bfloat16 or wider, within the bound.
No kernel may reach another device: no remote copies, remote signals or barrier semaphores. Data moves between devices by JAX's collectives and lax.ppermute only.
A program may use at most 128 MiB of HBM per device.

```python
import math
import jax
import jax.numpy as jnp
from jax import lax

CW = 1024
PIX = 16
LB = 128
KSEL = 3
D = 768
HEADS = 12
HD = 64
E = 512
OPT_DEV = 4
NQB = 8
NY = 128
NX = 512
NOPT = 1024
N_FREQ = 8
N_SY = 8
N_SX = 4


def draw_cube(key, part):
    key = jax.random.fold_in(key, 1)
    first, second, third = jax.random.split(key, 3)
    level = jax.random.uniform(first, (NY, NX), jnp.float32, 1.0, 4.0)
    noise = jax.random.normal(third, (CW, NY, NX), jnp.float32)
    spread = jnp.exp(jax.random.uniform(second, (NY, NX), jnp.float32, -1.2, 1.1))
    return (level[None] + spread[None] * noise).astype(jnp.bfloat16)


def draw_pattern(key, part):
    key = jax.random.fold_in(key, 2)
    shape = (N_SY, N_SX, N_FREQ, NQB, NQB)
    scores = jax.random.randint(key, shape, 0, 1 << 20) * NQB + lax.broadcasted_iota(jnp.int32, shape, 4)
    order = jnp.argsort(scores, axis=-1)
    return order[..., :KSEL].astype(jnp.int32)


def draw_match_ids(key, part):
    key = jax.random.fold_in(key, 3)
    shape = (N_SY, N_SX, N_FREQ)
    row_index = lax.broadcasted_iota(jnp.int32, shape, 0)
    col_index = lax.broadcasted_iota(jnp.int32, shape, 1)
    freq_index = lax.broadcasted_iota(jnp.int32, shape, 2)
    devices_all = N_SY * N_SX * N_FREQ
    device = freq_index * (N_SY * N_SX) + row_index * N_SX + col_index
    partner = (device + devices_all // 2) % devices_all
    offset = jax.random.randint(key, shape, 0, OPT_DEV)
    offset = jnp.where(partner == devices_all - 1, OPT_DEV - 1, offset)
    offset = jnp.where(partner == 0, 0, offset)
    return (partner * OPT_DEV + offset).astype(jnp.int32)


def draw_optical(key, part):
    key = jax.random.fold_in(key, 4)
    keys = jax.random.split(key, 4)
    devices_all = NOPT // OPT_DEV
    per_slice = devices_all // N_FREQ
    slice_dirs = jax.random.truncated_normal(keys[0], -3.0, 3.0, (N_FREQ, E), jnp.float32)
    device_dirs = jax.random.truncated_normal(keys[1], -3.0, 3.0, (devices_all, E), jnp.float32)
    direction = (jnp.repeat(slice_dirs, per_slice, axis=0) + device_dirs) * 0.7071
    direction = jnp.repeat(direction, OPT_DEV, axis=0)
    signs = jax.random.randint(keys[2], (NOPT, 1), 0, 2).astype(jnp.float32) * 2.0 - 1.0
    noise = jax.random.truncated_normal(keys[3], -4.0, 4.0, (NOPT, E), jnp.float32)
    amplitude = 3.0
    return (noise + amplitude * signs * direction).astype(jnp.bfloat16)


def centred(key, dims, width, reach, dtype=jnp.bfloat16):
    entries = width * jax.random.normal(key, dims, jnp.float32)
    return jnp.clip(entries, min=-reach, max=reach).astype(dtype)


def setup_inputs(seed: int = 0) -> dict:
    seeds = jax.random.split(jax.random.key(seed), 16)
    cube = draw_cube(jax.random.fold_in(seeds[15], 71), 0)
    pos_embed = centred(seeds[1], (CW, D), 0.5, 3.0)
    w_in = centred(seeds[2], (PIX * PIX, D), (PIX * PIX) ** -0.5, 0.375)
    norm_gain = jnp.clip(1.0 + 0.1 * jax.random.normal(seeds[3], (D,), jnp.float32), 0.5, 1.5)
    w_query = centred(seeds[4], (D, D), D ** -0.5, 0.21875)
    w_key = centred(seeds[5], (D, D), D ** -0.5, 0.21875)
    w_value = centred(seeds[6], (D, D), D ** -0.5, 0.21875)
    w_out = centred(seeds[7], (D, D), D ** -0.5, 0.21875)
    attn_scale = jnp.clip(jnp.exp(jax.random.uniform(seeds[8], (HEADS,), jnp.float32, math.log(3.0), math.log(30.0))), 3.0, 30.0)
    w_proj = centred(seeds[9], (D, E), D ** -0.5, 0.21875)
    mix_weight = centred(seeds[10], (3, 3, E), 0.4, 2.0, jnp.float32)
    optical = draw_optical(jax.random.fold_in(seeds[15], 71), 0)
    logit_scale = jnp.clip(jnp.exp(jax.random.uniform(seeds[12], (1,), jnp.float32, math.log(40.0), math.log(50.0))), 40.0, 50.0)
    pattern = draw_pattern(jax.random.fold_in(seeds[15], 71), 0)
    match_ids = draw_match_ids(jax.random.fold_in(seeds[15], 71), 0)
    return {"cube": cube, "pos_embed": pos_embed, "w_in": w_in, "norm_gain": norm_gain, "w_query": w_query, "w_key": w_key, "w_value": w_value, "w_out": w_out, "attn_scale": attn_scale, "w_proj": w_proj, "mix_weight": mix_weight, "optical": optical, "logit_scale": logit_scale, "pattern": pattern, "match_ids": match_ids}


def block_layer(spectrum, choose, pos_embed, w_in, norm_gain, w_query, w_key, w_value, w_out, attn_scale, w_proj):
    values = spectrum.astype(jnp.float32)
    centre = lax.optimization_barrier(jnp.mean(values, axis=0))
    spread = lax.optimization_barrier(jnp.mean(jnp.square(values - centre), axis=0))
    unit_spec = ((values - centre) / jnp.sqrt(spread + 1e-05)).astype(jnp.bfloat16)
    tokens = jnp.dot(unit_spec, w_in, preferred_element_type=jnp.float32) + pos_embed.astype(jnp.float32)
    square_mean = lax.optimization_barrier(jnp.mean(tokens * tokens, axis=-1, keepdims=True))
    normed = (tokens / jnp.sqrt(square_mean + 1e-06) * norm_gain).astype(jnp.bfloat16)

    def unit_heads(weight):
        projected = jnp.dot(normed, weight, preferred_element_type=jnp.float32).reshape(CW, HEADS, HD)
        length = lax.optimization_barrier(jnp.sum(projected * projected, axis=-1, keepdims=True))
        return (projected / jnp.sqrt(length + 1e-06)).astype(jnp.bfloat16).reshape(NQB, LB, HEADS, HD)
    queries = unit_heads(w_query)
    key_blocks = unit_heads(w_key)
    value_blocks = jnp.dot(normed, w_value, preferred_element_type=jnp.float32).astype(jnp.bfloat16).reshape(NQB, LB, HEADS, HD)
    chosen_keys = jnp.take(key_blocks, choose, axis=0).reshape(NQB, KSEL * LB, HEADS, HD)
    chosen_values = jnp.take(value_blocks, choose, axis=0).reshape(NQB, KSEL * LB, HEADS, HD)
    scores = jnp.einsum('qlhd,qmhd->qhlm', queries.astype(jnp.float32), chosen_keys.astype(jnp.float32))
    scores = scores * attn_scale[None, :, None, None]
    highest = lax.optimization_barrier(jnp.max(scores, axis=-1, keepdims=True))
    weights = jnp.exp(scores - highest)
    probs = (weights / lax.optimization_barrier(jnp.sum(weights, axis=-1, keepdims=True))).astype(jnp.bfloat16)
    heads_out = jnp.einsum('qhlm,qmhd->qlhd', probs.astype(jnp.float32), chosen_values.astype(jnp.float32))
    heads_out = heads_out.astype(jnp.bfloat16).reshape(CW, D)
    layer = tokens + jnp.dot(heads_out, w_out, preferred_element_type=jnp.float32)
    pooled = lax.optimization_barrier(jnp.mean(layer, axis=0)).astype(jnp.bfloat16)
    projected = jnp.dot(pooled[None, :], w_proj, preferred_element_type=jnp.float32)[0]
    return (layer.astype(jnp.bfloat16), projected)

def reference(cube, pos_embed, w_in, norm_gain, w_query, w_key, w_value, w_out, attn_scale, w_proj, mix_weight, optical, logit_scale, pattern, match_ids):
    blocks = N_SY * N_SX * N_FREQ
    spectra = cube.reshape(CW, N_SY, PIX, N_SX, N_FREQ, PIX).transpose(1, 3, 4, 0, 2, 5).reshape(blocks, CW, PIX * PIX)
    choices_all = pattern.reshape(blocks, NQB, KSEL).astype(jnp.int32)

    def per_block(item):
        return block_layer(item[0], item[1], pos_embed, w_in, norm_gain, w_query, w_key, w_value, w_out, attn_scale, w_proj)
    layers, projs = lax.map(per_block, (spectra, choices_all))
    layer_out = layers.reshape(N_SY, N_SX, N_FREQ, CW, D)
    plane = projs.reshape(N_SY, N_SX * N_FREQ, E)
    padded = jnp.pad(plane, ((1, 1), (1, 1), (0, 0)))
    mixed = jnp.zeros((N_SY, N_SX * N_FREQ, E), jnp.float32)
    for row_off in range(3):
        for col_off in range(3):
            mixed = mixed + mix_weight[row_off, col_off] * padded[row_off:row_off + N_SY, col_off:col_off + N_SX * N_FREQ]
    embed = mixed.reshape(N_SY, N_SX, N_FREQ, E)
    flat = mixed.reshape(blocks, E)
    unit = (flat / jnp.sqrt(lax.optimization_barrier(jnp.sum(flat * flat, axis=-1, keepdims=True)) + 1e-06)).astype(jnp.bfloat16)
    optical_f = optical.astype(jnp.float32)
    optical_unit = (optical_f / jnp.sqrt(lax.optimization_barrier(jnp.sum(optical_f * optical_f, axis=-1, keepdims=True)) + 1e-06)).astype(jnp.bfloat16)
    logits = jnp.dot(unit, optical_unit.T, preferred_element_type=jnp.float32) * logit_scale[0]
    highest = lax.optimization_barrier(jnp.max(logits, axis=-1))
    log_total = jnp.log(lax.optimization_barrier(jnp.sum(jnp.exp(logits - highest[:, None]), axis=-1))) + highest
    positive = jnp.take_along_axis(logits, match_ids.reshape(blocks, 1).astype(jnp.int32), axis=1)[:, 0]
    block_loss = (log_total - positive).reshape(N_SY, N_SX, N_FREQ)
    return (layer_out, embed, block_loss)
```

```python
import functools

import jax
import jax.numpy as jnp
from jax import lax
from jax.experimental import pallas as pl
from jax.experimental.pallas import tpu as pltpu
from jax.sharding import PartitionSpec as P

LB = 128
KSEL = 3
HEADS = 12
HD = 64
PAIRS = HEADS // 2
LOG2E = 1.4426950408889634

F32 = jnp.float32
BF16 = jnp.bfloat16
MIB = 1024 * 1024

SMEM = pl.BlockSpec(memory_space=pltpu.SMEM)
VMEM = pl.BlockSpec(memory_space=pltpu.VMEM)
ANY = pl.BlockSpec(memory_space=pl.ANY)


def dot(a, b):
    return jnp.dot(a, b, preferred_element_type=F32)


def dot_last(a, b):
    return lax.dot_general(a, b, (((1,), (1,)), ((), ())), preferred_element_type=F32)


def pack_kernel(place_ref, cube_ref, optical_ref, near_ref, far_ref, unit_ref, wide_ref):
    chans, side, columns = cube_ref.shape
    nfreq = columns // side
    half = nfreq // 2
    mine = place_ref[0]
    wide_ref[...] = cube_ref[...].astype(F32).reshape(chans * side, columns)
    for r in range(side):
        turned = wide_ref[pl.ds(r, chans, stride=side), :].T.astype(BF16)
        at = slice(r * side, (r + 1) * side)
        for y in range(half):
            d = (y - mine) & (half - 1)
            low = turned[y * side : (y + 1) * side, :]
            high = turned[(half + y) * side : (half + y + 1) * side, :]
            near_ref[d, at, :] = jnp.where(mine < half, low, high)
            far_ref[d, at, :] = jnp.where(mine < half, high, low)
    optical = optical_ref[...].astype(F32)
    unit = (optical * lax.rsqrt(jnp.sum(optical * optical, axis=-1, keepdims=True) + 1e-06)).astype(BF16)
    unit_ref[...] = jnp.concatenate([unit[:, q * LB : (q + 1) * LB] for q in range(unit.shape[1] // LB)], axis=0)


def merge_kernel(near_ref, far_ref, *refs):
    pixels = near_ref.shape[1]
    unit_refs, out_refs = refs[:4], refs[4:]
    rows = unit_refs[0].shape[0]
    for d, out_ref in enumerate(out_refs, 1):
        out_ref[:pixels, :] = near_ref[d]
        out_ref[pixels : 2 * pixels, :] = far_ref[d]
        for n, unit_ref in enumerate(unit_refs):
            out_ref[2 * pixels + n * rows : 2 * pixels + (n + 1) * rows, :] = unit_ref[...]


def load_kernel(pos_hbm, w_in_hbm, wq_hbm, wk_hbm, wv_hbm, pos_ref, w_in_ref, wq_ref, wkt_ref, wv_ref, wk_ref, sems):
    copies = [
        pltpu.make_async_copy(source, target, sems.at[n])
        for n, (source, target) in enumerate(
            [(wk_hbm, wk_ref), (w_in_hbm, w_in_ref), (pos_hbm, pos_ref), (wq_hbm, wq_ref), (wv_hbm, wv_ref)]
        )
    ]
    for copy in copies:
        copy.start()
    copies[0].wait()
    wkt_ref[...] = wk_ref[...].T
    for copy in copies[1:]:
        copy.wait()


def project_kernel(
    place_ref, near_ref, far_ref, one_ref, two_ref, three_ref, gain_ref, pos_ref, w_in_ref, wq_ref, wkt_ref, wv_ref,
    tokens_ref, q_ref, kt_ref, v_ref, sum_ref,
):
    chans = pos_ref.shape[0]
    pixels, width = w_in_ref.shape
    half = chans // LB // 2

    mine = place_ref[0]
    same, other = mine & half, half - (mine & half)
    pieces, blocks = [], []
    for d, ref in enumerate((None, one_ref, two_ref, three_ref)):
        source = (mine - d) & (half - 1)
        pieces.append(near_ref.at[0] if d == 0 else ref.at[:pixels])
        blocks.append(same + source)
        pieces.append(far_ref.at[0] if d == 0 else ref.at[pixels : 2 * pixels])
        blocks.append(other + source)

    total = pieces[0][...].astype(F32)
    for piece in pieces[1:]:
        total += piece[...].astype(F32)
    centre = jnp.sum(total, axis=1, keepdims=True) * (1.0 / chans)
    total = jnp.zeros((pixels, LB), F32)
    for piece in pieces:
        gap = piece[...].astype(F32) - centre
        total += gap * gap
    inverse = lax.rsqrt(jnp.sum(total, axis=1, keepdims=True) * (1.0 / chans) + 1e-05)

    row = lax.broadcasted_iota(jnp.int32, (256, 256), 0) // HD
    col = lax.broadcasted_iota(jnp.int32, (256, 256), 1) // HD
    same_head = jnp.where(row == col, 1.0, 0.0).astype(BF16)

    per = 2
    token_sum = jnp.zeros((1, width), F32)
    for i in range(0, len(pieces), per):
        places = [pl.ds(pl.multiple_of(b * LB, LB), LB) for b in blocks[i : i + per]]
        unit = jnp.concatenate(
            [((piece[...].astype(F32) - centre) * inverse).astype(BF16) for piece in pieces[i : i + per]], axis=1
        )
        tokens = lax.dot_general(unit, w_in_ref[...], (((0,), (0,)), ((), ())), preferred_element_type=F32)
        tokens += jnp.concatenate([pos_ref[at, :] for at in places], axis=0).astype(F32)
        square_mean = jnp.mean(tokens * tokens, axis=-1, keepdims=True)
        normed = (tokens * lax.rsqrt(square_mean + 1e-06) * gain_ref[...]).astype(BF16)
        token_sum += jnp.sum(tokens, axis=0, keepdims=True)
        for n, at in enumerate(places):
            tokens_ref[at, :] = tokens[n * LB : (n + 1) * LB]
        for c in range(width // 256):
            part = slice(c * 256, (c + 1) * 256)
            q = dot(normed, wq_ref[:, part])
            squares = q * q
            high = squares.astype(BF16)
            low = (squares - high.astype(F32)).astype(BF16)
            length = dot(high, same_head) + dot(low, same_head)
            q = (q * lax.rsqrt(length + 1e-06)).astype(BF16)
            for n, at in enumerate(places):
                q_ref[at, part] = q[n * LB : (n + 1) * LB]
        kt = dot_last(wkt_ref[...], normed)
        kt = kt.reshape(HEADS, HD, per * LB)
        length = jnp.sum(kt * kt, axis=1, keepdims=True)
        kt = (kt * lax.rsqrt(length + 1e-06)).astype(BF16).reshape(width, per * LB)
        v = dot(normed, wv_ref[...]).astype(BF16)
        for n, at in enumerate(places):
            kt_ref[blocks[i + n]] = kt[:, n * LB : (n + 1) * LB]
            v_ref[at, :] = v[n * LB : (n + 1) * LB]
    sum_ref[...] = token_sum


def attend_kernel(
    pattern_ref, scale_ref, q_ref, kt_ref, v_ref, sum_ref, wo_hbm, wproj_hbm,
    heads_ref, proj_ref,
    wo_ref, wproj_ref, sems,
):
    chans, width = q_ref.shape
    nblocks = chans // LB
    copies = [
        pltpu.make_async_copy(wo_hbm, wo_ref, sems.at[0]),
        pltpu.make_async_copy(wproj_hbm, wproj_ref, sems.at[1]),
    ]
    for copy in copies:
        copy.start()

    lower = lax.broadcasted_iota(jnp.int32, (KSEL * LB, LB), 1) < HD
    ones = jnp.ones((KSEL * LB, LB), BF16)
    zeros = jnp.zeros((KSEL * LB, LB), BF16)
    sums = jnp.concatenate([jnp.where(lower, ones, zeros), jnp.where(lower, zeros, ones)], axis=0)
    blank = jnp.zeros((HD, KSEL * LB), BF16)

    def attend(b, heads_sum):
        at = pl.ds(pl.multiple_of(b * LB, LB), LB)
        chosen = [pattern_ref[b, j] for j in range(KSEL)]
        parts = []
        for p in range(PAIRS):
            part = slice(p * LB, (p + 1) * LB)
            kt = jnp.concatenate([kt_ref[c, part, :] for c in chosen], axis=1)
            keys = jnp.concatenate(
                [jnp.concatenate([kt[:HD], blank], axis=0), jnp.concatenate([blank, kt[HD:]], axis=0)], axis=1
            )
            scores = dot(q_ref[at, part], keys)
            half = KSEL * LB
            weights = jnp.concatenate(
                [
                    jnp.exp2(scores[:, :half] * (scale_ref[2 * p] * LOG2E)).astype(BF16),
                    jnp.exp2(scores[:, half:] * (scale_ref[2 * p + 1] * LOG2E)).astype(BF16),
                ],
                axis=1,
            )
            v = jnp.concatenate([v_ref[pl.ds(pl.multiple_of(c * LB, LB), LB), part] for c in chosen], axis=0)
            values = jnp.concatenate([jnp.where(lower, v, zeros), jnp.where(lower, zeros, v)], axis=0)
            both = dot(weights, jnp.concatenate([values, sums], axis=1))
            out = (both[:, :LB] / both[:, LB:]).astype(BF16)
            heads_ref[at, part] = out
            parts.append(jnp.sum(out.astype(F32), axis=0, keepdims=True))
        return heads_sum + jnp.concatenate(parts, axis=1)

    heads_sum = lax.fori_loop(0, nblocks, attend, jnp.zeros((1, width), F32))

    heads_mean = heads_sum * (1.0 / chans)
    first = heads_mean.astype(BF16)
    rest = heads_mean - first.astype(F32)
    second = rest.astype(BF16)
    third = (rest - second.astype(F32)).astype(BF16)
    rows = jnp.concatenate([first, second, third, jnp.zeros((13, width), BF16)], axis=0)
    for copy in copies:
        copy.wait()
    mixed = jnp.sum(dot(rows, wo_ref[...]), axis=0, keepdims=True)
    pooled = (sum_ref[...] * (1.0 / chans) + mixed).astype(BF16)
    pooled = jnp.broadcast_to(pooled, (16, width))
    proj_ref[...] = dot(pooled, wproj_ref[...])[:1]


def spread_kernel(place_ref, proj_ref, even_ref, odd_ref, mix_ref, first_ref, own_ref, second_ref):
    column_odd, row_odd = place_ref[0] & 1 != 0, place_ref[1] & 1 != 0
    before = jnp.where(column_odd, even_ref[...], odd_ref[...])
    after = jnp.where(column_odd, odd_ref[...], even_ref[...])
    down, own, up = (
        mix_ref[a, 0:1] * before + mix_ref[a, 1:2] * proj_ref[...] + mix_ref[a, 2:3] * after for a in range(3)
    )
    own_ref[...] = own
    first_ref[...] = jnp.where(row_odd, up, down)
    second_ref[...] = jnp.where(row_odd, down, up)


def loss_kernel(sizes, place_ref, scale_ref, target_ref, first_ref, own_ref, second_ref, *refs):
    nfreq, nsy, nsx, held = sizes
    optical_refs, (embed_ref, loss_ref) = refs[:nsx], refs[nsx:]
    mixed = first_ref[...] + own_ref[...] + second_ref[...]
    embed_ref[...] = mixed
    unit = (mixed * lax.rsqrt(jnp.sum(mixed * mixed) + 1e-06)).astype(BF16)
    quarters = mixed.shape[1] // LB
    unit = jnp.concatenate(
        [unit[:, q * LB : (q + 1) * LB] for q in range(quarters)] + [jnp.zeros((16 - quarters, LB), BF16)], axis=0
    )
    rows = optical_refs[0].shape[0]
    place = lax.broadcasted_iota(jnp.int32, (1, rows), 1)
    first = (place // held) % quarters == 0
    parts = []
    for ref in optical_refs:
        products = dot_last(unit, ref[...])
        logits = products[0:1]
        for q in range(1, quarters):
            logits = logits + pltpu.roll(products[q : q + 1], rows - q * held, 1)
        parts.append(logits)
    logits = jnp.concatenate(parts, axis=1) * scale_ref[0]
    place = lax.broadcasted_iota(jnp.int32, logits.shape, 1)
    logits = jnp.where(jnp.concatenate([first] * nsx, axis=1), logits, -jnp.inf)
    highest = jnp.max(logits, axis=1, keepdims=True)
    summed = jnp.sum(jnp.exp(logits - highest), axis=1, keepdims=True)

    half = nfreq // 2
    target = target_ref[0]
    k = target % held
    device = target // held
    sx = (place_ref[2] - device) & (nsx - 1)
    sy = (device // nsx) % nsy
    sy = (((place_ref[1] >> 1) - (sy >> 1)) & (nsy // 2 - 1)) * 2 + ((place_ref[1] ^ sy) & 1)
    f = device // (nsx * nsy)
    flipped = jnp.where((f ^ place_ref[0]) & half != 0, 1, 0)
    y = (place_ref[0] - f) & (half - 1)
    where = ((((sx * 2 + flipped) * half + y) * nsy + sy) * quarters) * held + k
    positive = jnp.sum(jnp.where(place == where, logits, 0.0), axis=1, keepdims=True)
    loss_ref[...] = jnp.log(summed) + highest - positive


def vmem(mib):
    return pltpu.CompilerParams(vmem_limit_bytes=mib * MIB)


def load(pos_embed, w_in, w_query, w_key, w_value):
    weights = (pos_embed, w_in, w_query, w_key, w_value)
    return pl.pallas_call(
        load_kernel,
        out_shape=tuple(jax.ShapeDtypeStruct(w.shape, BF16) for w in weights),
        in_specs=[ANY] * 5,
        out_specs=(VMEM,) * 5,
        scratch_shapes=[pltpu.VMEM(w_key.shape, BF16), pltpu.SemaphoreType.DMA((5,))],
        compiler_params=vmem(16),
        cost_estimate=pl.CostEstimate(flops=0, bytes_accessed=14_000_000, transcendentals=0),
    )(*weights)


def project(place, pieces, norm_gain, weights):
    chans, width = weights[0].shape
    return pl.pallas_call(
        project_kernel,
        out_shape=(
            jax.ShapeDtypeStruct((chans, width), F32),
            jax.ShapeDtypeStruct((chans, width), BF16),
            jax.ShapeDtypeStruct((chans // LB, width, LB), BF16),
            jax.ShapeDtypeStruct((chans, width), BF16),
            jax.ShapeDtypeStruct((1, width), F32),
        ),
        in_specs=[SMEM] + [VMEM] * (len(pieces) + 6),
        out_specs=(VMEM,) * 5,
        compiler_params=vmem(32),
        cost_estimate=pl.CostEstimate(flops=8_000_000_000, bytes_accessed=12_000_000, transcendentals=1_000_000),
    )(place, *pieces, norm_gain.reshape(1, width), *weights)


def attend(choose, attn_scale, queries, keys, values, token_sum, w_out, w_proj):
    chans, width = queries.shape
    return pl.pallas_call(
        attend_kernel,
        out_shape=(
            jax.ShapeDtypeStruct((chans, width), BF16),
            jax.ShapeDtypeStruct((1, w_proj.shape[1]), F32),
        ),
        in_specs=[SMEM, SMEM, VMEM, VMEM, VMEM, VMEM, ANY, ANY],
        out_specs=(VMEM, VMEM),
        scratch_shapes=[
            pltpu.VMEM(w_out.shape, BF16), pltpu.VMEM(w_proj.shape, BF16), pltpu.SemaphoreType.DMA((2,))
        ],
        compiler_params=vmem(40),
        cost_estimate=pl.CostEstimate(flops=8_000_000_000, bytes_accessed=8_000_000, transcendentals=5_000_000),
    )(choose, attn_scale, queries, keys, values, token_sum, w_out, w_proj)


def pairs(length, begin):
    return [pair for i in range(begin, length - 1, 2) for pair in ((i, i + 1), (i + 1, i))]


def column_pairs(begin, nfreq, nsx):
    def index(c):
        return c % nfreq * nsx + c // nfreq

    return [(index(a), index(b)) for a, b in pairs(nfreq * nsx, begin)]


def per_device(
    cube, pos_embed, w_in, norm_gain, w_query, w_key, w_value, w_out, attn_scale, w_proj, mix_weight, optical,
    logit_scale, pattern, match_ids,
):
    nfreq, nsy, nsx = (lax.axis_size(axis) for axis in ("freq", "sy", "sx"))
    half = nfreq // 2
    place = jnp.stack([lax.axis_index(axis) for axis in ("freq", "sy", "sx")]).astype(jnp.int32)
    local_chans, side = cube.shape[:2]
    pixels = side * side
    held, width = optical.shape
    rows = held * width // LB

    def steps_y(array, d):
        return lax.ppermute(array, "freq", [(i, i // half * half + (i + d) % half) for i in range(nfreq)])

    def other_half(array):
        return lax.ppermute(array, "freq", [(i, (i + half) % nfreq) for i in range(nfreq)])

    blocks = jax.ShapeDtypeStruct((half, pixels, local_chans), BF16)
    near, far, unit = pl.pallas_call(
        pack_kernel,
        out_shape=(blocks, blocks, jax.ShapeDtypeStruct((rows, LB), BF16)),
        in_specs=[SMEM, VMEM, VMEM],
        out_specs=(VMEM,) * 3,
        scratch_shapes=[pltpu.VMEM((local_chans * side, cube.shape[2]), F32)],
        compiler_params=vmem(8),
    )(place, cube, optical)
    far = other_half(far)
    far, *weights = lax.optimization_barrier((far, pos_embed, w_in, w_query, w_key, w_value))
    unit = jnp.concatenate([unit, lax.ppermute(unit, "sy", [(i, i ^ 1) for i in range(nsy)])], axis=0)
    units = [unit] + [lax.ppermute(unit, "sy", [(i, (i + 2 * d) % nsy) for i in range(nsy)]) for d in range(1, nsy // 2)]
    sent = pl.pallas_call(
        merge_kernel,
        out_shape=(jax.ShapeDtypeStruct((2 * pixels + nsy * rows, LB), BF16),) * (half - 1),
        in_specs=[VMEM] * (2 + len(units)),
        out_specs=(VMEM,) * (half - 1),
        compiler_params=vmem(8),
    )(near, far, *units)
    taken = [steps_y(array, d) for d, array in enumerate(sent, 1)]

    candidates = jnp.concatenate(units + [array[2 * pixels :] for array in taken], axis=0)
    others = other_half(candidates)
    tokens, queries, keys, values, token_sum = project(
        place, [near, far] + taken, norm_gain, load(*weights)
    )
    others, token_sum = lax.optimization_barrier((others, token_sum))
    candidates = jnp.concatenate([candidates, others], axis=0)
    candidates = [candidates] + [
        lax.ppermute(candidates, "sx", [(i, (i + d) % nsx) for i in range(nsx)]) for d in range(1, nsx)
    ]
    choose = pattern.reshape(pattern.shape[3], pattern.shape[4])
    heads_out, proj = attend(choose, attn_scale, queries, keys, values, token_sum, w_out, w_proj)
    proj, *candidates = lax.optimization_barrier((proj, *candidates))
    layer_out = (tokens + dot(heads_out, w_out)).astype(BF16)

    even = lax.ppermute(proj, ("freq", "sx"), column_pairs(0, nfreq, nsx))
    odd = lax.ppermute(proj, ("freq", "sx"), column_pairs(1, nfreq, nsx))
    line = jax.ShapeDtypeStruct((1, width), F32)
    first, own, second = pl.pallas_call(
        spread_kernel,
        out_shape=(line,) * 3,
        in_specs=[SMEM] + [VMEM] * 4,
        out_specs=(VMEM,) * 3,
        compiler_params=vmem(4),
    )(place, proj, even, odd, mix_weight)
    first = lax.ppermute(first, "sy", pairs(nsy, 0))
    second = lax.ppermute(second, "sy", pairs(nsy, 1))
    embed, loss = pl.pallas_call(
        functools.partial(loss_kernel, (nfreq, nsy, nsx, held)),
        out_shape=(line, jax.ShapeDtypeStruct((1, 1), F32)),
        in_specs=[SMEM] * 3 + [VMEM] * (3 + nsx),
        out_specs=(VMEM, VMEM),
        compiler_params=vmem(8),
    )(place, logit_scale, match_ids.reshape(1), first, own, second, *candidates)
    return (
        layer_out.reshape((1, 1, 1) + layer_out.shape),
        embed.reshape(1, 1, 1, width),
        loss.reshape(1, 1, 1),
    )


def solution(mesh):
    in_specs = (
        P("freq", "sy", "sx"), P(), P(), P(), P(), P(), P(), P(), P(), P(), P(),
        P(("freq", "sy", "sx"), None), P(), P("sy", "sx", "freq", None, None), P("sy", "sx", "freq"),
    )
    out_specs = (
        P("sy", "sx", "freq", None, None),
        P("sy", "sx", "freq", None),
        P("sy", "sx", "freq"),
    )
    return jax.shard_map(per_device, mesh=mesh, in_specs=in_specs, out_specs=out_specs, check_vma=False)
```

```python
import functools

import jax
import jax.numpy as jnp
from jax import lax
from jax.experimental import pallas as pl
from jax.experimental.pallas import tpu as pltpu
from jax.sharding import PartitionSpec as P

LB = 128
KSEL = 3
HEADS = 12
HD = 64
PAIRS = HEADS // 2
LOG2E = 1.4426950408889634

F32 = jnp.float32
BF16 = jnp.bfloat16
MIB = 1024 * 1024

SMEM = pl.BlockSpec(memory_space=pltpu.SMEM)
VMEM = pl.BlockSpec(memory_space=pltpu.VMEM)
ANY = pl.BlockSpec(memory_space=pl.ANY)


def dot(a, b):
    return jnp.dot(a, b, preferred_element_type=F32)


def dot_last(a, b):
    return lax.dot_general(a, b, (((1,), (1,)), ((), ())), preferred_element_type=F32)


def pack_kernel(place_ref, cube_ref, optical_ref, near_ref, far_ref, unit_ref, wide_ref):
    chans, side, columns = cube_ref.shape
    nfreq = columns // side
    half = nfreq // 2
    mine = place_ref[0]
    wide_ref[...] = cube_ref[...].astype(F32).reshape(chans * side, columns)
    for r in range(side):
        turned = wide_ref[pl.ds(r, chans, stride=side), :].T.astype(BF16)
        at = slice(r * side, (r + 1) * side)
        for y in range(half):
            d = (y - mine) & (half - 1)
            low = turned[y * side : (y + 1) * side, :]
            high = turned[(half + y) * side : (half + y + 1) * side, :]
            near_ref[d, at, :] = jnp.where(mine < half, low, high)
            far_ref[d, at, :] = jnp.where(mine < half, high, low)
    optical = optical_ref[...].astype(F32)
    unit = (optical * lax.rsqrt(jnp.sum(optical * optical, axis=-1, keepdims=True) + 1e-06)).astype(BF16)
    unit_ref[...] = jnp.concatenate([unit[:, q * LB : (q + 1) * LB] for q in range(unit.shape[1] // LB)], axis=0)


def merge_kernel(near_ref, far_ref, *refs):
    pixels = near_ref.shape[1]
    unit_refs, out_refs = refs[: -(near_ref.shape[0] - 1)], refs[-(near_ref.shape[0] - 1) :]
    for d, out_ref in enumerate(out_refs, 1):
        out_ref[:pixels, :] = near_ref[d]
        out_ref[pixels : 2 * pixels, :] = far_ref[d]
        row = 2 * pixels
        for unit_ref in unit_refs:
            out_ref[row : row + unit_ref.shape[0], :] = unit_ref[...]
            row += unit_ref.shape[0]


def load_kernel(turned, *refs):
    count = len(turned)
    sources, targets, scratches, sems = refs[:count], refs[count : 2 * count], refs[2 * count : -1], refs[-1]
    landing = list(scratches)
    places = [landing.pop(0) if turn else target for turn, target in zip(turned, targets)]
    copies = [pltpu.make_async_copy(a, b, sems.at[n]) for n, (a, b) in enumerate(zip(sources, places))]
    for copy in copies:
        copy.start()
    for copy, turn, place, target in zip(copies, turned, places, targets):
        copy.wait()
        if turn:
            target[...] = place[...].T


def project_kernel(
    place_ref, near_ref, far_ref, one_ref, two_ref, three_ref, gain_ref, pos_ref, w_in_ref, wq_ref, wkt_ref, wv_ref,
    tokens_ref, q_ref, kt_ref, v_ref, sum_ref,
):
    chans = pos_ref.shape[0]
    pixels, width = w_in_ref.shape
    half = chans // LB // 2

    mine = place_ref[0]
    same, other = mine & half, half - (mine & half)
    pieces, blocks = [], []
    for d, ref in enumerate((None, one_ref, two_ref, three_ref)):
        source = (mine - d) & (half - 1)
        pieces.append(near_ref.at[0] if d == 0 else ref.at[:pixels])
        blocks.append(same + source)
        pieces.append(far_ref.at[0] if d == 0 else ref.at[pixels : 2 * pixels])
        blocks.append(other + source)

    total = pieces[0][...].astype(F32)
    for piece in pieces[1:]:
        total += piece[...].astype(F32)
    centre = jnp.sum(total, axis=1, keepdims=True) * (1.0 / chans)
    total = jnp.zeros((pixels, LB), F32)
    for piece in pieces:
        gap = piece[...].astype(F32) - centre
        total += gap * gap
    inverse = lax.rsqrt(jnp.sum(total, axis=1, keepdims=True) * (1.0 / chans) + 1e-05)

    per = len(pieces)
    token_sum = jnp.zeros((1, width), F32)
    for i in range(0, len(pieces), per):
        places = [pl.ds(pl.multiple_of(b * LB, LB), LB) for b in blocks[i : i + per]]
        unit = jnp.concatenate(
            [((piece[...].astype(F32) - centre) * inverse).astype(BF16) for piece in pieces[i : i + per]], axis=1
        )
        tokens = lax.dot_general(unit, w_in_ref[...], (((0,), (0,)), ((), ())), preferred_element_type=F32)
        tokens += jnp.concatenate([pos_ref[at, :] for at in places], axis=0).astype(F32)
        square_mean = jnp.mean(tokens * tokens, axis=-1, keepdims=True)
        normed = (tokens * lax.rsqrt(square_mean + 1e-06) * gain_ref[...]).astype(BF16)
        token_sum += jnp.sum(tokens, axis=0, keepdims=True)
        for n, at in enumerate(places):
            tokens_ref[at, :] = tokens[n * LB : (n + 1) * LB]
        qt = lax.dot_general(wq_ref[...], normed, (((0,), (1,)), ((), ())), preferred_element_type=F32)
        qt = qt.reshape(HEADS, HD, per * LB)
        length = jnp.sum(qt * qt, axis=1, keepdims=True)
        q = (qt * lax.rsqrt(length + 1e-06)).astype(BF16).reshape(width, per * LB).T
        for n, at in enumerate(places):
            q_ref[at, :] = q[n * LB : (n + 1) * LB]
        kt = dot_last(wkt_ref[...], normed)
        kt = kt.reshape(HEADS, HD, per * LB)
        length = jnp.sum(kt * kt, axis=1, keepdims=True)
        kt = (kt * lax.rsqrt(length + 1e-06)).astype(BF16).reshape(width, per * LB)
        v = dot(normed, wv_ref[...]).astype(BF16)
        for n, at in enumerate(places):
            kt_ref[blocks[i + n]] = kt[:, n * LB : (n + 1) * LB]
            v_ref[at, :] = v[n * LB : (n + 1) * LB]
    sum_ref[...] = token_sum


def attend_kernel(
    pattern_ref, scale_ref, q_ref, kt_ref, v_ref, sum_ref, wo_hbm, wproj_hbm,
    heads_ref, proj_ref, wo_ref,
    wproj_ref, sems,
):
    chans, width = q_ref.shape
    nblocks = chans // LB
    copies = [
        pltpu.make_async_copy(wo_hbm, wo_ref, sems.at[0]),
        pltpu.make_async_copy(wproj_hbm, wproj_ref, sems.at[1]),
    ]
    for copy in copies:
        copy.start()

    lower = lax.broadcasted_iota(jnp.int32, (KSEL * LB, LB), 1) < HD
    ones = jnp.ones((KSEL * LB, LB), BF16)
    zeros = jnp.zeros((KSEL * LB, LB), BF16)
    sums = jnp.concatenate([jnp.where(lower, ones, zeros), jnp.where(lower, zeros, ones)], axis=0)
    blank = jnp.zeros((HD, KSEL * LB), BF16)

    def attend(b, heads_sum):
        at = pl.ds(pl.multiple_of(b * LB, LB), LB)
        chosen = [pattern_ref[b, j] for j in range(KSEL)]
        parts = []
        for p in range(PAIRS):
            part = slice(p * LB, (p + 1) * LB)
            kt = jnp.concatenate([kt_ref[c, part, :] for c in chosen], axis=1)
            keys = jnp.concatenate(
                [jnp.concatenate([kt[:HD], blank], axis=0), jnp.concatenate([blank, kt[HD:]], axis=0)], axis=1
            )
            scores = dot(q_ref[at, part], keys)
            half = KSEL * LB
            weights = jnp.concatenate(
                [
                    jnp.exp2(scores[:, :half] * (scale_ref[2 * p] * LOG2E)).astype(BF16),
                    jnp.exp2(scores[:, half:] * (scale_ref[2 * p + 1] * LOG2E)).astype(BF16),
                ],
                axis=1,
            )
            v = jnp.concatenate([v_ref[pl.ds(pl.multiple_of(c * LB, LB), LB), part] for c in chosen], axis=0)
            values = jnp.concatenate([jnp.where(lower, v, zeros), jnp.where(lower, zeros, v)], axis=0)
            both = dot(weights, jnp.concatenate([values, sums], axis=1))
            out = (both[:, :LB] / both[:, LB:]).astype(BF16)
            heads_ref[at, part] = out
            parts.append(jnp.sum(out.astype(F32), axis=0, keepdims=True))
        return heads_sum + jnp.concatenate(parts, axis=1)

    heads_sum = lax.fori_loop(0, nblocks, attend, jnp.zeros((1, width), F32), unroll=True)

    heads_mean = heads_sum * (1.0 / chans)
    first = heads_mean.astype(BF16)
    rest = heads_mean - first.astype(F32)
    second = rest.astype(BF16)
    third = (rest - second.astype(F32)).astype(BF16)
    rows = jnp.concatenate([first, second, third, jnp.zeros((13, width), BF16)], axis=0)
    for copy in copies:
        copy.wait()
    mixed = jnp.sum(dot(rows, wo_ref[...]), axis=0, keepdims=True)
    pooled = (sum_ref[...] * (1.0 / chans) + mixed).astype(BF16)
    pooled = jnp.broadcast_to(pooled, (16, width))
    proj_ref[...] = dot(pooled, wproj_ref[...])[:1]


def layer_kernel(tokens_ref, heads_ref, wo_ref, layer_hbm, done_ref, rounded_ref, sems):
    rows = tokens_ref.shape[0] // sems.shape[0]
    copies = []
    for n in range(sems.shape[0]):
        at = pl.ds(n * rows, rows)
        rounded_ref[at, :] = (tokens_ref[at, :] + dot(heads_ref[at, :], wo_ref[...])).astype(BF16)
        copies.append(pltpu.make_async_copy(rounded_ref.at[at], layer_hbm.at[at], sems.at[n]))
        copies[-1].start()
    done_ref[...] = jnp.zeros(done_ref.shape, F32)
    for copy in copies:
        copy.wait()


def spread_kernel(place_ref, proj_ref, even_ref, odd_ref, mix_ref, done_ref, first_ref, own_ref, second_ref):
    column_odd, row_odd = place_ref[0] & 1 != 0, place_ref[1] & 1 != 0
    before = jnp.where(column_odd, even_ref[...], odd_ref[...])
    after = jnp.where(column_odd, odd_ref[...], even_ref[...])
    down, own, up = (
        mix_ref[a, 0:1] * before + mix_ref[a, 1:2] * proj_ref[...] + mix_ref[a, 2:3] * after for a in range(3)
    )
    own_ref[...] = own
    first_ref[...] = jnp.where(row_odd, up, down)
    second_ref[...] = jnp.where(row_odd, down, up)


def loss_kernel(sizes, place_ref, scale_ref, target_ref, first_ref, own_ref, second_ref, *refs):
    nfreq, nsy, nsx, held = sizes
    optical_refs, (embed_ref, loss_ref) = refs[:nsx], refs[nsx:]
    mixed = first_ref[...] + own_ref[...] + second_ref[...]
    embed_ref[...] = mixed
    unit = (mixed * lax.rsqrt(jnp.sum(mixed * mixed) + 1e-06)).astype(BF16)
    quarters = mixed.shape[1] // LB
    unit = jnp.concatenate(
        [unit[:, q * LB : (q + 1) * LB] for q in range(quarters)] + [jnp.zeros((16 - quarters, LB), BF16)], axis=0
    )
    rows = optical_refs[0].shape[0]
    place = lax.broadcasted_iota(jnp.int32, (1, rows), 1)
    first = (place // held) % quarters == 0
    parts = []
    for ref in optical_refs:
        products = dot_last(unit, ref[...])
        logits = products[0:1]
        for q in range(1, quarters):
            logits = logits + pltpu.roll(products[q : q + 1], rows - q * held, 1)
        parts.append(logits)
    logits = jnp.concatenate(parts, axis=1) * scale_ref[0]
    place = lax.broadcasted_iota(jnp.int32, logits.shape, 1)
    logits = jnp.where(jnp.concatenate([first] * nsx, axis=1), logits, -jnp.inf)
    highest = jnp.max(logits, axis=1, keepdims=True)
    summed = jnp.sum(jnp.exp(logits - highest), axis=1, keepdims=True)

    half = nfreq // 2
    target = target_ref[0]
    k = target % held
    device = target // held
    sx = (place_ref[2] - device) & (nsx - 1)
    sy = (device // nsx) % nsy
    sy = (((place_ref[1] >> 1) - (sy >> 1)) & (nsy // 2 - 1)) * 2 + ((place_ref[1] ^ sy) & 1)
    f = device // (nsx * nsy)
    flipped = jnp.where((f ^ place_ref[0]) & half != 0, 1, 0)
    y = (place_ref[0] - f) & (half - 1)
    where = ((((sx * 2 + flipped) * half + y) * nsy + sy) * quarters) * held + k
    positive = jnp.sum(jnp.where(place == where, logits, 0.0), axis=1, keepdims=True)
    loss_ref[...] = jnp.log(summed) + highest - positive


def vmem(mib):
    return pltpu.CompilerParams(vmem_limit_bytes=mib * MIB)


def load(turned, *weights):
    return pl.pallas_call(
        functools.partial(load_kernel, turned),
        out_shape=tuple(jax.ShapeDtypeStruct(w.shape, BF16) for w in weights),
        in_specs=[ANY] * len(weights),
        out_specs=(VMEM,) * len(weights),
        scratch_shapes=[pltpu.VMEM(w.shape, BF16) for w, turn in zip(weights, turned) if turn]
        + [pltpu.SemaphoreType.DMA((len(weights),))],
        compiler_params=vmem(12),
        cost_estimate=pl.CostEstimate(flops=0, bytes_accessed=sum(4 * w.size for w in weights), transcendentals=0),
    )(*weights)


def project(place, pieces, norm_gain, weights):
    chans, width = weights[0].shape
    return pl.pallas_call(
        project_kernel,
        out_shape=(
            jax.ShapeDtypeStruct((chans, width), F32),
            jax.ShapeDtypeStruct((chans, width), BF16),
            jax.ShapeDtypeStruct((chans // LB, width, LB), BF16),
            jax.ShapeDtypeStruct((chans, width), BF16),
            jax.ShapeDtypeStruct((1, width), F32),
        ),
        in_specs=[SMEM] + [VMEM] * (len(pieces) + 6),
        out_specs=(VMEM,) * 5,
        compiler_params=vmem(32),
        cost_estimate=pl.CostEstimate(flops=8_000_000_000, bytes_accessed=12_000_000, transcendentals=1_000_000),
    )(place, *pieces, norm_gain.reshape(1, width), *weights)


def attend(choose, attn_scale, queries, keys, values, token_sum, w_out, w_proj):
    chans, width = queries.shape
    return pl.pallas_call(
        attend_kernel,
        out_shape=(
            jax.ShapeDtypeStruct((chans, width), BF16),
            jax.ShapeDtypeStruct((1, w_proj.shape[1]), F32),
            jax.ShapeDtypeStruct(w_out.shape, BF16),
        ),
        in_specs=[SMEM, SMEM, VMEM, VMEM, VMEM, VMEM, ANY, ANY],
        out_specs=(VMEM,) * 3,
        scratch_shapes=[pltpu.VMEM(w_proj.shape, BF16), pltpu.SemaphoreType.DMA((2,))],
        compiler_params=vmem(40),
        cost_estimate=pl.CostEstimate(flops=8_000_000_000, bytes_accessed=8_000_000, transcendentals=5_000_000),
    )(choose, attn_scale, queries, keys, values, token_sum, w_out, w_proj)


def pairs(length, begin):
    return [pair for i in range(begin, length - 1, 2) for pair in ((i, i + 1), (i + 1, i))]


def column_pairs(begin, nfreq, nsx):
    def index(c):
        return c % nfreq * nsx + c // nfreq

    return [(index(a), index(b)) for a, b in pairs(nfreq * nsx, begin)]


def per_device(
    cube, pos_embed, w_in, norm_gain, w_query, w_key, w_value, w_out, attn_scale, w_proj, mix_weight, optical,
    logit_scale, pattern, match_ids,
):
    nfreq, nsy, nsx = (lax.axis_size(axis) for axis in ("freq", "sy", "sx"))
    half = nfreq // 2
    place = jnp.stack([lax.axis_index(axis) for axis in ("freq", "sy", "sx")]).astype(jnp.int32)
    local_chans, side = cube.shape[:2]
    pixels = side * side
    held, width = optical.shape
    rows = held * width // LB

    def steps_y(array, d):
        return lax.ppermute(array, "freq", [(i, i // half * half + (i + d) % half) for i in range(nfreq)])

    def other_half(array):
        return lax.ppermute(array, "freq", [(i, (i + half) % nfreq) for i in range(nfreq)])

    blocks = jax.ShapeDtypeStruct((half, pixels, local_chans), BF16)
    near, far, unit = pl.pallas_call(
        pack_kernel,
        out_shape=(blocks, blocks, jax.ShapeDtypeStruct((rows, LB), BF16)),
        in_specs=[SMEM, VMEM, VMEM],
        out_specs=(VMEM,) * 3,
        scratch_shapes=[pltpu.VMEM((local_chans * side, cube.shape[2]), F32)],
        compiler_params=vmem(8),
    )(place, cube, optical)
    far = other_half(far)
    unit = jnp.concatenate([unit, lax.ppermute(unit, "sy", [(i, i ^ 1) for i in range(nsy)])], axis=0)
    units = [unit] + [lax.ppermute(unit, "sy", [(i, (i + 2 * d) % nsy) for i in range(nsy)]) for d in range(1, nsy // 2)]
    far, *weights = lax.optimization_barrier((far, pos_embed, w_in, w_query, w_key, w_value))
    weights = load((False, False, False, True, False), *weights)
    sent = pl.pallas_call(
        merge_kernel,
        out_shape=(jax.ShapeDtypeStruct((2 * pixels + nsy * rows, LB), BF16),) * (half - 1),
        in_specs=[VMEM] * (2 + len(units)),
        out_specs=(VMEM,) * (half - 1),
        compiler_params=vmem(8),
    )(near, far, *units)
    taken = [steps_y(array, d) for d, array in enumerate(sent, 1)]
    candidates = jnp.concatenate(units + [array[2 * pixels :] for array in taken], axis=0)
    others = other_half(candidates)
    tokens, queries, keys, values, token_sum = project(place, [near, far] + taken, norm_gain, weights)
    others, token_sum = lax.optimization_barrier((others, token_sum))
    candidates = jnp.concatenate([candidates, others], axis=0)
    candidates = [candidates] + [
        lax.ppermute(candidates, "sx", [(i, (i + d) % nsx) for i in range(nsx)]) for d in range(1, nsx)
    ]
    choose = pattern.reshape(pattern.shape[3], pattern.shape[4])
    heads_out, proj, held_out = attend(choose, attn_scale, queries, keys, values, token_sum, w_out, w_proj)
    layer_out, done = pl.pallas_call(
        layer_kernel,
        out_shape=(jax.ShapeDtypeStruct(tokens.shape, BF16), jax.ShapeDtypeStruct((8, LB), F32)),
        in_specs=[VMEM] * 3,
        out_specs=(ANY, VMEM),
        scratch_shapes=[pltpu.VMEM(tokens.shape, BF16), pltpu.SemaphoreType.DMA((4,))],
        compiler_params=vmem(16),
        cost_estimate=pl.CostEstimate(flops=2_000_000_000, bytes_accessed=8_000_000, transcendentals=0),
    )(tokens, heads_out, held_out)

    even = lax.ppermute(proj, ("freq", "sx"), column_pairs(0, nfreq, nsx))
    odd = lax.ppermute(proj, ("freq", "sx"), column_pairs(1, nfreq, nsx))
    line = jax.ShapeDtypeStruct((1, width), F32)
    first, own, second = pl.pallas_call(
        spread_kernel,
        out_shape=(line,) * 3,
        in_specs=[SMEM] + [VMEM] * 5,
        out_specs=(VMEM,) * 3,
        compiler_params=vmem(4),
    )(place, proj, even, odd, mix_weight, done)
    first = lax.ppermute(first, "sy", pairs(nsy, 0))
    second = lax.ppermute(second, "sy", pairs(nsy, 1))
    embed, loss = pl.pallas_call(
        functools.partial(loss_kernel, (nfreq, nsy, nsx, held)),
        out_shape=(line, jax.ShapeDtypeStruct((1, 1), F32)),
        in_specs=[SMEM] * 3 + [VMEM] * (3 + nsx),
        out_specs=(VMEM, VMEM),
        compiler_params=vmem(8),
    )(place, logit_scale, match_ids.reshape(1), first, own, second, *candidates)
    return (
        layer_out.reshape((1, 1, 1) + layer_out.shape),
        embed.reshape(1, 1, 1, width),
        loss.reshape(1, 1, 1),
    )


def solution(mesh):
    in_specs = (
        P("freq", "sy", "sx"), P(), P(), P(), P(), P(), P(), P(), P(), P(), P(),
        P(("freq", "sy", "sx"), None), P(), P("sy", "sx", "freq", None, None), P("sy", "sx", "freq"),
    )
    out_specs = (
        P("sy", "sx", "freq", None, None),
        P("sy", "sx", "freq", None),
        P("sy", "sx", "freq"),
    )
    return jax.shard_map(per_device, mesh=mesh, in_specs=in_specs, out_specs=out_specs, check_vma=False)
```

```python
import functools

import jax
import jax.numpy as jnp
from jax import lax
from jax.experimental import pallas as pl
from jax.experimental.pallas import tpu as pltpu
from jax.sharding import PartitionSpec as P

LB = 128
KSEL = 3
HEADS = 12
HD = 64
PAIRS = HEADS // 2
LOG2E = 1.4426950408889634

F32 = jnp.float32
BF16 = jnp.bfloat16
MIB = 1024 * 1024

SMEM = pl.BlockSpec(memory_space=pltpu.SMEM)
VMEM = pl.BlockSpec(memory_space=pltpu.VMEM)
ANY = pl.BlockSpec(memory_space=pl.ANY)


def dot(a, b):
    return jnp.dot(a, b, preferred_element_type=F32)


def dot_last(a, b):
    return lax.dot_general(a, b, (((1,), (1,)), ((), ())), preferred_element_type=F32)


def pack_kernel(place_ref, cube_ref, near_ref, far_ref, wide_ref):
    chans, side, columns = cube_ref.shape
    nfreq = columns // side
    half = nfreq // 2
    mine = place_ref[0]
    wide_ref[...] = cube_ref[...].astype(F32).reshape(chans * side, columns)
    for r in range(side):
        turned = wide_ref[pl.ds(r, chans, stride=side), :].T.astype(BF16)
        at = slice(r * side, (r + 1) * side)
        for y in range(half):
            d = (y - mine) & (half - 1)
            low = turned[y * side : (y + 1) * side, :]
            high = turned[(half + y) * side : (half + y + 1) * side, :]
            near_ref[d, at, :] = jnp.where(mine < half, low, high)
            far_ref[d, at, :] = jnp.where(mine < half, high, low)


def unit_kernel(after_ref, optical_ref, unit_ref):
    del after_ref
    optical = optical_ref[...].astype(F32)
    unit = (optical * lax.rsqrt(jnp.sum(optical * optical, axis=-1, keepdims=True) + 1e-06)).astype(BF16)
    unit_ref[...] = jnp.concatenate([unit[:, q * LB : (q + 1) * LB] for q in range(unit.shape[1] // LB)], axis=0)


def merge_kernel(near_ref, far_ref, *refs):
    pixels = near_ref.shape[1]
    unit_refs, out_refs = refs[: -(near_ref.shape[0] - 1)], refs[-(near_ref.shape[0] - 1) :]
    for d, out_ref in enumerate(out_refs, 1):
        out_ref[:pixels, :] = near_ref[d]
        out_ref[pixels : 2 * pixels, :] = far_ref[d]
        row = 2 * pixels
        for unit_ref in unit_refs:
            out_ref[row : row + unit_ref.shape[0], :] = unit_ref[...]
            row += unit_ref.shape[0]


def load_kernel(turned, *refs):
    count = len(turned)
    sources, targets, scratches, sems = refs[:count], refs[count : 2 * count], refs[2 * count : -1], refs[-1]
    landing = list(scratches)
    places = [landing.pop(0) if turn else target for turn, target in zip(turned, targets)]
    copies = [pltpu.make_async_copy(a, b, sems.at[n]) for n, (a, b) in enumerate(zip(sources, places))]
    for copy in copies:
        copy.start()
    for copy, turn, place, target in zip(copies, turned, places, targets):
        copy.wait()
        if turn:
            target[...] = place[...].T


def project_kernel(
    place_ref, near_ref, far_ref, one_ref, two_ref, three_ref, gain_ref, pos_ref, w_in_ref, wq_ref, wkt_ref, wv_ref,
    tokens_ref, q_ref, kt_ref, v_ref, sum_ref,
):
    chans = pos_ref.shape[0]
    pixels, width = w_in_ref.shape
    half = chans // LB // 2

    mine = place_ref[0]
    same, other = mine & half, half - (mine & half)
    pieces, blocks = [], []
    for d, ref in enumerate((None, one_ref, two_ref, three_ref)):
        source = (mine - d) & (half - 1)
        pieces.append(near_ref.at[0] if d == 0 else ref.at[:pixels])
        blocks.append(same + source)
        pieces.append(far_ref.at[0] if d == 0 else ref.at[pixels : 2 * pixels])
        blocks.append(other + source)

    total = pieces[0][...].astype(F32)
    for piece in pieces[1:]:
        total += piece[...].astype(F32)
    centre = jnp.sum(total, axis=1, keepdims=True) * (1.0 / chans)
    total = jnp.zeros((pixels, LB), F32)
    for piece in pieces:
        gap = piece[...].astype(F32) - centre
        total += gap * gap
    inverse = lax.rsqrt(jnp.sum(total, axis=1, keepdims=True) * (1.0 / chans) + 1e-05)

    per = len(pieces)
    token_sum = jnp.zeros((1, width), F32)
    for i in range(0, len(pieces), per):
        places = [pl.ds(pl.multiple_of(b * LB, LB), LB) for b in blocks[i : i + per]]
        unit = jnp.concatenate(
            [((piece[...].astype(F32) - centre) * inverse).astype(BF16) for piece in pieces[i : i + per]], axis=1
        )
        tokens = lax.dot_general(unit, w_in_ref[...], (((0,), (0,)), ((), ())), preferred_element_type=F32)
        tokens += jnp.concatenate([pos_ref[at, :] for at in places], axis=0).astype(F32)
        square_mean = jnp.mean(tokens * tokens, axis=-1, keepdims=True)
        normed = (tokens * lax.rsqrt(square_mean + 1e-06) * gain_ref[...].reshape(1, width)).astype(BF16)
        token_sum += jnp.sum(tokens, axis=0, keepdims=True)
        for n, at in enumerate(places):
            tokens_ref[at, :] = tokens[n * LB : (n + 1) * LB]
        qt = lax.dot_general(wq_ref[...], normed, (((0,), (1,)), ((), ())), preferred_element_type=F32)
        qt = qt.reshape(HEADS, HD, per * LB)
        length = jnp.sum(qt * qt, axis=1, keepdims=True)
        q = (qt * lax.rsqrt(length + 1e-06)).astype(BF16).reshape(width, per * LB).T
        for n, at in enumerate(places):
            q_ref[at, :] = q[n * LB : (n + 1) * LB]
        kt = dot_last(wkt_ref[...], normed)
        kt = kt.reshape(HEADS, HD, per * LB)
        length = jnp.sum(kt * kt, axis=1, keepdims=True)
        kt = (kt * lax.rsqrt(length + 1e-06)).astype(BF16).reshape(width, per * LB)
        v = dot(normed, wv_ref[...]).astype(BF16)
        for n, at in enumerate(places):
            kt_ref[blocks[i + n]] = kt[:, n * LB : (n + 1) * LB]
            v_ref[at, :] = v[n * LB : (n + 1) * LB]
    sum_ref[...] = token_sum


def attend_kernel(
    pattern_ref, scale_ref, q_ref, kt_ref, v_ref, sum_ref, wo_hbm, wproj_hbm,
    heads_ref, proj_ref, wo_ref,
    wproj_ref, sems,
):
    chans, width = q_ref.shape
    nblocks = chans // LB
    copies = [
        pltpu.make_async_copy(wo_hbm, wo_ref, sems.at[0]),
        pltpu.make_async_copy(wproj_hbm, wproj_ref, sems.at[1]),
    ]
    for copy in copies:
        copy.start()

    lower = lax.broadcasted_iota(jnp.int32, (KSEL * LB, LB), 1) < HD
    ones = jnp.ones((KSEL * LB, LB), BF16)
    zeros = jnp.zeros((KSEL * LB, LB), BF16)
    sums = jnp.concatenate([jnp.where(lower, ones, zeros), jnp.where(lower, zeros, ones)], axis=0)
    blank = jnp.zeros((HD, KSEL * LB), BF16)

    def attend(b, heads_sum):
        at = pl.ds(pl.multiple_of(b * LB, LB), LB)
        chosen = [pattern_ref[0, 0, 0, b, j] for j in range(KSEL)]
        parts = []
        for p in range(PAIRS):
            part = slice(p * LB, (p + 1) * LB)
            kt = jnp.concatenate([kt_ref[c, part, :] for c in chosen], axis=1)
            keys = jnp.concatenate(
                [jnp.concatenate([kt[:HD], blank], axis=0), jnp.concatenate([blank, kt[HD:]], axis=0)], axis=1
            )
            scores = dot(q_ref[at, part], keys)
            half = KSEL * LB
            weights = jnp.concatenate(
                [
                    jnp.exp2(scores[:, :half] * (scale_ref[2 * p] * LOG2E)).astype(BF16),
                    jnp.exp2(scores[:, half:] * (scale_ref[2 * p + 1] * LOG2E)).astype(BF16),
                ],
                axis=1,
            )
            v = jnp.concatenate([v_ref[pl.ds(pl.multiple_of(c * LB, LB), LB), part] for c in chosen], axis=0)
            values = jnp.concatenate([jnp.where(lower, v, zeros), jnp.where(lower, zeros, v)], axis=0)
            both = dot(weights, jnp.concatenate([values, sums], axis=1))
            out = (both[:, :LB] / both[:, LB:]).astype(BF16)
            heads_ref[at, part] = out
            parts.append(jnp.sum(out.astype(F32), axis=0, keepdims=True))
        return heads_sum + jnp.concatenate(parts, axis=1)

    heads_sum = lax.fori_loop(0, nblocks, attend, jnp.zeros((1, width), F32), unroll=True)

    heads_mean = heads_sum * (1.0 / chans)
    first = heads_mean.astype(BF16)
    rest = heads_mean - first.astype(F32)
    second = rest.astype(BF16)
    third = (rest - second.astype(F32)).astype(BF16)
    rows = jnp.concatenate([first, second, third, jnp.zeros((13, width), BF16)], axis=0)
    for copy in copies:
        copy.wait()
    mixed = jnp.sum(dot(rows, wo_ref[...]), axis=0, keepdims=True)
    pooled = (sum_ref[...] * (1.0 / chans) + mixed).astype(BF16)
    pooled = jnp.broadcast_to(pooled, (16, width))
    proj_ref[...] = dot(pooled, wproj_ref[...])[:1]


def layer_kernel(tokens_ref, heads_ref, wo_ref, layer_hbm, done_ref, rounded_ref, sems):
    rows = tokens_ref.shape[0] // sems.shape[0]
    copies = []
    for n in range(sems.shape[0]):
        at = pl.ds(n * rows, rows)
        rounded_ref[at, :] = (tokens_ref[at, :] + dot(heads_ref[at, :], wo_ref[...])).astype(BF16)
        copies.append(pltpu.make_async_copy(rounded_ref.at[at], layer_hbm.at[at], sems.at[n]))
        copies[-1].start()
    done_ref[...] = jnp.zeros(done_ref.shape, F32)
    for copy in copies:
        copy.wait()


def spread_kernel(place_ref, proj_ref, even_ref, odd_ref, mix_ref, done_ref, first_ref, own_ref, second_ref):
    column_odd, row_odd = place_ref[0] & 1 != 0, place_ref[1] & 1 != 0
    before = jnp.where(column_odd, even_ref[...], odd_ref[...])
    after = jnp.where(column_odd, odd_ref[...], even_ref[...])
    down, own, up = (
        mix_ref[a, 0:1] * before + mix_ref[a, 1:2] * proj_ref[...] + mix_ref[a, 2:3] * after for a in range(3)
    )
    own_ref[...] = own
    first_ref[...] = jnp.where(row_odd, up, down)
    second_ref[...] = jnp.where(row_odd, down, up)


def loss_kernel(sizes, place_ref, scale_ref, target_ref, first_ref, own_ref, second_ref, *refs):
    nfreq, nsy, nsx, held = sizes
    optical_refs, (embed_ref, loss_ref) = refs[:-2], refs[-2:]
    mixed = first_ref[...] + own_ref[...] + second_ref[...]
    embed_ref[...] = mixed
    unit = (mixed * lax.rsqrt(jnp.sum(mixed * mixed) + 1e-06)).astype(BF16)
    quarters = mixed.shape[1] // LB
    unit = jnp.concatenate(
        [unit[:, q * LB : (q + 1) * LB] for q in range(quarters)] + [jnp.zeros((16 - quarters, LB), BF16)], axis=0
    )
    rows = optical_refs[0].shape[0]
    place = lax.broadcasted_iota(jnp.int32, (1, rows), 1)
    first = (place // held) % quarters == 0
    parts = []
    for ref in optical_refs:
        products = dot_last(unit, ref[...])
        logits = products[0:1]
        for q in range(1, quarters):
            logits = logits + pltpu.roll(products[q : q + 1], rows - q * held, 1)
        parts.append(logits)
    logits = jnp.concatenate(parts, axis=1) * scale_ref[0]
    place = lax.broadcasted_iota(jnp.int32, logits.shape, 1)
    logits = jnp.where(jnp.concatenate([first] * len(parts), axis=1), logits, -jnp.inf)
    highest = jnp.max(logits, axis=1, keepdims=True)
    summed = jnp.sum(jnp.exp(logits - highest), axis=1, keepdims=True)

    half = nfreq // 2
    target = target_ref[0]
    k = target % held
    device = target // held
    sx = (place_ref[2] - device) & (nsx - 1)
    sy = (device // nsx) % nsy
    core = (place_ref[1] ^ sy) & 1
    sy = ((place_ref[1] >> 1) - (sy >> 1)) & (nsy // 2 - 1)
    f = device // (nsx * nsy)
    flipped = jnp.where((f ^ place_ref[0]) & half != 0, 1, 0)
    y = (place_ref[0] - f) & (half - 1)
    where = (((((core * nsx + sx) * 2 + flipped) * half + y) * (nsy // 2) + sy) * quarters) * held + k
    positive = jnp.sum(jnp.where(place == where, logits, 0.0), axis=1, keepdims=True)
    loss_ref[...] = jnp.log(summed) + highest - positive


def vmem(mib):
    return pltpu.CompilerParams(vmem_limit_bytes=mib * MIB)


def load(turned, *weights):
    return pl.pallas_call(
        functools.partial(load_kernel, turned),
        out_shape=tuple(jax.ShapeDtypeStruct(w.shape, BF16) for w in weights),
        in_specs=[ANY] * len(weights),
        out_specs=(VMEM,) * len(weights),
        scratch_shapes=[pltpu.VMEM(w.shape, BF16) for w, turn in zip(weights, turned) if turn]
        + [pltpu.SemaphoreType.DMA((len(weights),))],
        compiler_params=vmem(12),
        cost_estimate=pl.CostEstimate(flops=0, bytes_accessed=sum(4 * w.size for w in weights), transcendentals=0),
    )(*weights)


def project(place, pieces, norm_gain, weights):
    chans, width = weights[0].shape
    return pl.pallas_call(
        project_kernel,
        out_shape=(
            jax.ShapeDtypeStruct((chans, width), F32),
            jax.ShapeDtypeStruct((chans, width), BF16),
            jax.ShapeDtypeStruct((chans // LB, width, LB), BF16),
            jax.ShapeDtypeStruct((chans, width), BF16),
            jax.ShapeDtypeStruct((1, width), F32),
        ),
        in_specs=[SMEM] + [VMEM] * (len(pieces) + 6),
        out_specs=(VMEM,) * 5,
        compiler_params=vmem(32),
        cost_estimate=pl.CostEstimate(flops=8_000_000_000, bytes_accessed=12_000_000, transcendentals=1_000_000),
    )(place, *pieces, norm_gain, *weights)


def attend(choose, attn_scale, queries, keys, values, token_sum, w_out, w_proj):
    chans, width = queries.shape
    return pl.pallas_call(
        attend_kernel,
        out_shape=(
            jax.ShapeDtypeStruct((chans, width), BF16),
            jax.ShapeDtypeStruct((1, w_proj.shape[1]), F32),
            jax.ShapeDtypeStruct(w_out.shape, BF16),
        ),
        in_specs=[SMEM, SMEM, VMEM, VMEM, VMEM, VMEM, ANY, ANY],
        out_specs=(VMEM,) * 3,
        scratch_shapes=[pltpu.VMEM(w_proj.shape, BF16), pltpu.SemaphoreType.DMA((2,))],
        compiler_params=vmem(40),
        cost_estimate=pl.CostEstimate(flops=8_000_000_000, bytes_accessed=8_000_000, transcendentals=5_000_000),
    )(choose, attn_scale, queries, keys, values, token_sum, w_out, w_proj)


def pairs(length, begin):
    return [pair for i in range(begin, length - 1, 2) for pair in ((i, i + 1), (i + 1, i))]


def column_pairs(begin, nfreq, nsx):
    def index(c):
        return c % nfreq * nsx + c // nfreq

    return [(index(a), index(b)) for a, b in pairs(nfreq * nsx, begin)]


def per_device(
    cube, pos_embed, w_in, norm_gain, w_query, w_key, w_value, w_out, attn_scale, w_proj, mix_weight, optical,
    logit_scale, pattern, match_ids,
):
    nfreq, nsy, nsx = (lax.axis_size(axis) for axis in ("freq", "sy", "sx"))
    half = nfreq // 2
    place = jnp.stack([lax.axis_index(axis) for axis in ("freq", "sy", "sx")]).astype(jnp.int32)
    local_chans, side = cube.shape[:2]
    pixels = side * side
    held, width = optical.shape
    rows = held * width // LB

    def steps_y(array, d):
        return lax.ppermute(array, "freq", [(i, i // half * half + (i + d) % half) for i in range(nfreq)])

    def other_half(array):
        return lax.ppermute(array, "freq", [(i, (i + half) % nfreq) for i in range(nfreq)])

    blocks = jax.ShapeDtypeStruct((half, pixels, local_chans), BF16)
    near, far = pl.pallas_call(
        pack_kernel,
        out_shape=(blocks, blocks),
        in_specs=[SMEM, VMEM],
        out_specs=(VMEM,) * 2,
        scratch_shapes=[pltpu.VMEM((local_chans * side, cube.shape[2]), F32)],
        compiler_params=vmem(8),
    )(place, cube)
    unit = pl.pallas_call(
        unit_kernel,
        out_shape=jax.ShapeDtypeStruct((rows, LB), BF16),
        in_specs=[VMEM] * 2,
        out_specs=VMEM,
        compiler_params=vmem(4),
    )(near, optical)
    far = other_half(far)
    units = [unit] + [lax.ppermute(unit, "sy", [(i, (i + 2 * d) % nsy) for i in range(nsy)]) for d in range(1, nsy // 2)]
    far, *weights = lax.optimization_barrier((far, pos_embed, w_in, w_query, w_key, w_value))
    weights = load((False, False, False, True, False), *weights)
    sent = pl.pallas_call(
        merge_kernel,
        out_shape=(jax.ShapeDtypeStruct((2 * pixels + nsy // 2 * rows, LB), BF16),) * (half - 1),
        in_specs=[VMEM] * (2 + len(units)),
        out_specs=(VMEM,) * (half - 1),
        compiler_params=vmem(8),
    )(near, far, *units)
    taken = [steps_y(array, d) for d, array in enumerate(sent, 1)]
    candidates = jnp.concatenate(units + [array[2 * pixels :] for array in taken], axis=0)
    others = other_half(candidates)
    tokens, queries, keys, values, token_sum = project(place, [near, far] + taken, norm_gain, weights)
    candidates = jnp.concatenate([candidates, others], axis=0)
    candidates = [candidates] + [
        lax.ppermute(candidates, "sx", [(i, (i + d) % nsx) for i in range(nsx)]) for d in range(1, nsx)
    ]
    heads_out, proj, held_out = attend(pattern, attn_scale, queries, keys, values, token_sum, w_out, w_proj)
    layer_out, done = pl.pallas_call(
        layer_kernel,
        out_shape=(jax.ShapeDtypeStruct(tokens.shape, BF16), jax.ShapeDtypeStruct((8, LB), F32)),
        in_specs=[VMEM] * 3,
        out_specs=(ANY, VMEM),
        scratch_shapes=[pltpu.VMEM(tokens.shape, BF16), pltpu.SemaphoreType.DMA((4,))],
        compiler_params=vmem(16),
        cost_estimate=pl.CostEstimate(flops=2_000_000_000, bytes_accessed=8_000_000, transcendentals=0),
    )(tokens, heads_out, held_out)
    even = lax.ppermute(proj, ("freq", "sx"), column_pairs(0, nfreq, nsx))
    odd = lax.ppermute(proj, ("freq", "sx"), column_pairs(1, nfreq, nsx))
    line = jax.ShapeDtypeStruct((1, width), F32)
    first, own, second = pl.pallas_call(
        spread_kernel,
        out_shape=(line,) * 3,
        in_specs=[SMEM] + [VMEM] * 5,
        out_specs=(VMEM,) * 3,
        compiler_params=vmem(4),
    )(place, proj, even, odd, mix_weight, done)
    own, *candidates = lax.optimization_barrier((own, *candidates))
    candidates = jnp.concatenate(candidates, axis=0)
    candidates = [candidates, lax.ppermute(candidates, "sy", pairs(nsy, 0))]

    first = lax.ppermute(first, "sy", pairs(nsy, 0))
    second = lax.ppermute(second, "sy", pairs(nsy, 1))
    embed, loss = pl.pallas_call(
        functools.partial(loss_kernel, (nfreq, nsy, nsx, held)),
        out_shape=(line, jax.ShapeDtypeStruct((1, 1), F32)),
        in_specs=[SMEM] * 3 + [VMEM] * (3 + len(candidates)),
        out_specs=(VMEM, VMEM),
        compiler_params=vmem(8),
    )(place, logit_scale, match_ids.reshape(1), first, own, second, *candidates)
    return (
        layer_out.reshape((1, 1, 1) + layer_out.shape),
        embed.reshape(1, 1, 1, width),
        loss.reshape(1, 1, 1),
    )


def solution(mesh):
    in_specs = (
        P("freq", "sy", "sx"), P(), P(), P(), P(), P(), P(), P(), P(), P(), P(),
        P(("freq", "sy", "sx"), None), P(), P("sy", "sx", "freq", None, None), P("sy", "sx", "freq"),
    )
    out_specs = (
        P("sy", "sx", "freq", None, None),
        P("sy", "sx", "freq", None),
        P("sy", "sx", "freq"),
    )
    return jax.shard_map(per_device, mesh=mesh, in_specs=in_specs, out_specs=out_specs, check_vma=False)
```
